32 devices in a mesh: pencil: 32 (over z, y, x, core).
Axes of the slice: x: 2, y: 2, z: 4, core: 2. Of those that a mesh axis runs over, the one named last changes fastest.
Arguments:
- coefficients: float32 [2, 8, 16384, 128], P(None, None, 'pencil'), may hold values from -6 to 6
- potential: float32 [256, 256, 256], P('pencil'), may hold values from -5 to 5
- slot_atom: int32 [2048], P('pencil'), may hold values from 0 to 511, as said below
- slot_count: int32 [32], P('pencil'), may hold values from 8 to 64, as said below
- point_offset: int32 [2048, 256], P('pencil'), may hold values from 0 to 524287
- proj_value: float32 [2048, 8, 256], P('pencil'), may hold values from -0.7 to 0.7
- proj_strength: float32 [512, 8], replicated, may hold values from 0.5 to 4
- proj_count: int32 [512], replicated, may hold values from 1 to 8
Outputs:
- applied_coefficients: float32 [2, 8, 16384, 128], P(None, None, 'pencil')
- projections: float32 [512, 128], P('pencil')
The draws below stay inside these ranges and needn't reach their ends.
Inputs may be any that keep to these rules, and one draw needn't show every extreme that they name: `slot_atom`: the home block of atom a is a // 16; the atom of every slot of block d has its home block within 2 of d modulo the number of blocks, so (a // 16 - d) modulo the number of blocks is at most 2 or at least the number of blocks minus 2. `slot_count`: some block uses all 64 slots.
All inputs are finite; a program needn't handle non-finite values.
Results may differ from the reference program's by a relative error of at most 0.00011.
Values sent between devices are 32-bit elements; how exact they have to be, the bound alone decides.
A program may use at most 512 MiB of HBM per device.

```python
import math
import jax
import jax.numpy as jnp
from jax import lax

GRID_SIDE = 256
WAVE_CUTOFF = 128
ZL = 8
BANDS = 8
ATOM_DEV = 16
ATOMS = 512
NPROJ = 8
SLOTS = 64
NPTS = 256
REACH = 2
N_PENCIL = 32


def draw_slot_atom(key, part):
    key_reach = jax.random.fold_in(key, 11)
    key_within = jax.random.fold_in(key, 12)
    count_all = N_PENCIL * SLOTS
    blocks = jnp.arange(count_all, dtype=jnp.int32) // SLOTS
    offsets = jax.random.randint(key_reach, (count_all,), -REACH, REACH + 1, dtype=jnp.int32)
    within = jax.random.randint(key_within, (count_all,), 0, ATOM_DEV, dtype=jnp.int32)
    offsets = offsets.at[0].set(0).at[count_all - 1].set(0)
    within = within.at[0].set(0).at[count_all - 1].set(ATOM_DEV - 1)
    home_block = (blocks + offsets) % N_PENCIL
    return (home_block * ATOM_DEV + within).astype(jnp.int32)


def draw_slot_count(key, part):
    key_base = jax.random.fold_in(key, 21)
    key_heavy = jax.random.fold_in(key, 22)
    key_pick = jax.random.fold_in(key, 23)
    base_count = jax.random.randint(key_base, (N_PENCIL,), SLOTS // 8, SLOTS // 2 + 1, dtype=jnp.int32)
    heavy_block = jax.random.randint(key_heavy, (N_PENCIL,), 0, 16, dtype=jnp.int32) == 0
    counts = jnp.where(heavy_block, SLOTS, base_count)
    chosen = jax.random.randint(key_pick, (), 0, N_PENCIL, dtype=jnp.int32)
    counts = counts.at[chosen].set(SLOTS).at[(chosen + 1) % N_PENCIL].set(SLOTS // 8)
    return counts.astype(jnp.int32)


def set_ends(entries, key, low, high):
    extent = entries.shape
    index_at = [jax.random.randint(jax.random.fold_in(key, axis), (), 0, extent[axis]) for axis in range(len(extent))]
    entries = entries.at[tuple(index_at)].set(low)
    longest = extent.index(max(extent))
    index_at[longest] = (index_at[longest] + 1) % extent[longest]
    return entries.at[tuple(index_at)].set(high)


def block_scale(rng, extent, pieces, low, largest):
    factor_of = 1.0
    for position, blocks in pieces:
        heights = jax.random.uniform(jax.random.fold_in(jax.random.fold_in(rng, 6), position), (blocks,), jnp.float32, low / len(pieces), largest / len(pieces))
        factor_of = factor_of * jnp.repeat(jnp.exp(heights), extent[position] // blocks).reshape((-1,) + (1,) * (len(extent) - 1 - position))
    return factor_of


def gaussian(stream_key, shape, deviation, reach, split=(), kind=jnp.bfloat16):
    factor_of = block_scale(stream_key, shape, split, -0.22, 0.18) if split else 1.0
    entries = jax.random.normal(stream_key, shape, jnp.float32) * deviation * factor_of
    return jnp.minimum(jnp.maximum(entries, -reach), reach).astype(kind)


def setup_inputs(seed: int = 0) -> dict:
    key_of = jax.random.split(jax.random.key(seed), 9)
    return {
        "coefficients": gaussian(key_of[0], (2, BANDS, WAVE_CUTOFF * WAVE_CUTOFF, WAVE_CUTOFF), 1.0, 6.0, ((2, 32),), jnp.float32),
        "potential": gaussian(key_of[1], (GRID_SIDE, GRID_SIDE, GRID_SIDE), 1.0, 5.0, ((0, 32),), jnp.float32),
        "slot_atom": draw_slot_atom(jax.random.fold_in(key_of[8], 71), 0),
        "slot_count": draw_slot_count(jax.random.fold_in(key_of[8], 71), 0),
        "point_offset": set_ends(jax.random.randint(key_of[4], (N_PENCIL * SLOTS, NPTS), 0, ZL * GRID_SIDE * GRID_SIDE), jax.random.fold_in(key_of[4], 1), 0, (ZL * GRID_SIDE * GRID_SIDE) - 1).astype(jnp.int32),
        "proj_value": gaussian(key_of[5], (N_PENCIL * SLOTS, NPROJ, NPTS), 0.12, 0.7, ((0, 32),), jnp.float32),
        "proj_strength": jnp.clip(jnp.exp(jax.random.uniform(key_of[6], (ATOMS, NPROJ), jnp.float32, math.log(0.5), math.log(4.0))), 0.5, 4.0),
        "proj_count": set_ends(jax.random.randint(key_of[7], (ATOMS,), 1, NPROJ + 1), jax.random.fold_in(key_of[7], 1), 1, NPROJ).astype(jnp.int32),
    }


def kinetic_table():
    frequency = jnp.arange(WAVE_CUTOFF, dtype=jnp.int32) - WAVE_CUTOFF // 2
    squared = (frequency * frequency).astype(jnp.float32)
    summed = squared[:, None, None] + squared[None, :, None] + squared[None, None, :]
    return (6.0 / (WAVE_CUTOFF * WAVE_CUTOFF)) * summed.reshape(WAVE_CUTOFF * WAVE_CUTOFF, WAVE_CUTOFF)


def reference(coefficients, potential, slot_atom, slot_count, point_offset, proj_value, proj_strength, proj_count):
    highest = lax.Precision.HIGHEST
    box_index = (jnp.arange(WAVE_CUTOFF, dtype=jnp.int32) - WAVE_CUTOFF // 2) % GRID_SIDE
    slot_all = N_PENCIL * SLOTS
    slot_block = jnp.arange(slot_all, dtype=jnp.int32) // SLOTS
    used_slot = (jnp.arange(slot_all, dtype=jnp.int32) % SLOTS) < slot_count[slot_block]
    cell_index = (slot_block[:, None] * (ZL * GRID_SIDE * GRID_SIDE) + point_offset).astype(jnp.int32)
    weights = jnp.where(used_slot[:, None, None], proj_value, jnp.zeros_like(proj_value))
    proj_mask = jnp.arange(NPROJ, dtype=jnp.int32)[None, :] < proj_count[:, None]
    slot_strength = proj_strength[slot_atom]
    kinetic = kinetic_table()
    potential_flat = potential.reshape(-1)

    def one_band(band_amplitudes):
        grid_real = jnp.zeros((GRID_SIDE, GRID_SIDE, GRID_SIDE), jnp.float32).at[box_index[:, None, None], box_index[None, :, None], box_index[None, None, :]].set(band_amplitudes[0].reshape(WAVE_CUTOFF, WAVE_CUTOFF, WAVE_CUTOFF))
        grid_imag = jnp.zeros((GRID_SIDE, GRID_SIDE, GRID_SIDE), jnp.float32).at[box_index[:, None, None], box_index[None, :, None], box_index[None, None, :]].set(band_amplitudes[1].reshape(WAVE_CUTOFF, WAVE_CUTOFF, WAVE_CUTOFF))
        field_grid = jnp.fft.ifftn(lax.complex(grid_real, grid_imag)) * ((GRID_SIDE ** 3) * (WAVE_CUTOFF ** -1.5))
        ordered = jnp.transpose(field_grid, (2, 1, 0)).reshape(-1)
        fields = jnp.stack([jnp.real(ordered), jnp.imag(ordered)])
        picked = fields[:, cell_index]
        partial_terms = jnp.einsum('cst,spt->scp', picked, weights, precision=highest)
        summed = jax.ops.segment_sum(partial_terms, slot_atom, num_segments=ATOMS)
        becp_band = jnp.where(proj_mask[:, None, :], summed, jnp.zeros_like(summed))
        energy = becp_band[slot_atom] * slot_strength[:, None, :]
        added = jnp.einsum('scp,spt->cst', energy, weights, precision=highest)
        projected = jnp.zeros_like(fields).at[:, cell_index].add(added)
        applied = potential_flat[None, :] * fields + projected
        grid_back = jnp.transpose(lax.complex(applied[0], applied[1]).reshape(GRID_SIDE, GRID_SIDE, GRID_SIDE), (2, 1, 0))
        spectrum = jnp.fft.fftn(grid_back) * (GRID_SIDE ** -1.5)
        kept = spectrum[box_index][:, box_index][:, :, box_index].reshape(WAVE_CUTOFF * WAVE_CUTOFF, WAVE_CUTOFF)
        result = jnp.stack([jnp.real(kept), jnp.imag(kept)]) + kinetic[None] * band_amplitudes
        return result, becp_band

    results, becps = lax.map(one_band, jnp.transpose(coefficients, (1, 0, 2, 3)))
    applied_coefficients = jnp.transpose(results, (1, 0, 2, 3))
    projections = jnp.transpose(becps, (1, 2, 0, 3)).reshape(ATOMS, 2 * BANDS * NPROJ)
    return applied_coefficients, projections
```

```python
import math

import jax
import jax.numpy as jnp
import ml_dtypes
import numpy as np
from jax import lax
from jax.experimental import pallas as pl
from jax.experimental.pallas import tpu as pltpu
from jax.sharding import PartitionSpec as P

GRID_SIDE = 256
WAVE_CUTOFF = 128
NPROJ = 8
REACH = 2


def passed_along(block, axis, distance):
    devices = range(lax.axis_size(axis))
    route = [((i - distance) % len(devices), i) for i in devices]
    return lax.ppermute(block, axis, route)


def phase_tables():
    frequency = jnp.arange(WAVE_CUTOFF, dtype=jnp.int32) - WAVE_CUTOFF // 2
    points = jnp.arange(GRID_SIDE, dtype=jnp.int32)
    turn_count = frequency[:, None] * points[None, :] % GRID_SIDE
    phase_angles = 2.0 * math.pi / GRID_SIDE * turn_count.astype(jnp.float32)
    return (jnp.cos(phase_angles), jnp.sin(phase_angles))


def complex_step(real_part, imag_part, full_pattern, table, factor):
    stacked = jnp.stack([real_part, imag_part])
    result = jnp.einsum(full_pattern, stacked, table, precision=lax.Precision.HIGHEST)
    return (factor * result[0], factor * result[1])


def forward_dim(real_part, imag_part, full_pattern, cosine_lookup, sine_lookup, factor):
    table = jnp.stack(
        [jnp.stack([cosine_lookup, sine_lookup]), jnp.stack([-sine_lookup, cosine_lookup])]
    )
    return complex_step(real_part, imag_part, full_pattern, table, factor)


def backward_dim(real_part, imag_part, full_pattern, cosine_lookup, sine_lookup, factor):
    table = jnp.stack(
        [jnp.stack([cosine_lookup, -sine_lookup]), jnp.stack([sine_lookup, cosine_lookup])]
    )
    return complex_step(real_part, imag_part, full_pattern, table, factor)


def columns_to_planes(band_amplitudes, cosine_lookup, sine_lookup):
    real_part, imag_part = forward_dim(
        band_amplitudes[0],
        band_amplitudes[1],
        "rchw,rowa->ocah",
        cosine_lookup,
        sine_lookup,
        WAVE_CUTOFF ** (-0.5),
    )
    return jnp.stack([real_part, imag_part])


def planes_to_grid(incoming_pieces, cosine_lookup, sine_lookup):
    shape_now = incoming_pieces.shape
    real_part = incoming_pieces[0].reshape(shape_now[1], shape_now[2], WAVE_CUTOFF, WAVE_CUTOFF)
    imag_part = incoming_pieces[1].reshape(shape_now[1], shape_now[2], WAVE_CUTOFF, WAVE_CUTOFF)
    real_part, imag_part = forward_dim(
        real_part, imag_part, "rbzkj,rojy->obzky", cosine_lookup, sine_lookup, WAVE_CUTOFF ** (-0.5)
    )
    return forward_dim(
        real_part, imag_part, "rbzky,rokx->obzyx", cosine_lookup, sine_lookup, WAVE_CUTOFF ** (-0.5)
    )


def grid_to_planes(real_part, imag_part, cosine_lookup, sine_lookup):
    real_part, imag_part = backward_dim(
        real_part, imag_part, "rbzyx,rokx->obzyk", cosine_lookup, sine_lookup, GRID_SIDE ** (-0.5)
    )
    real_part, imag_part = backward_dim(
        real_part, imag_part, "rbzyk,rojy->obzkj", cosine_lookup, sine_lookup, GRID_SIDE ** (-0.5)
    )
    shape_now = real_part.shape
    return jnp.stack(
        [
            real_part.reshape(shape_now[0], shape_now[1], WAVE_CUTOFF * WAVE_CUTOFF),
            imag_part.reshape(shape_now[0], shape_now[1], WAVE_CUTOFF * WAVE_CUTOFF),
        ]
    )


def planes_to_columns(incoming_pieces, cosine_lookup, sine_lookup):
    real_part, imag_part = backward_dim(
        incoming_pieces[0],
        incoming_pieces[1],
        "runv,rotn->ouvt",
        cosine_lookup,
        sine_lookup,
        GRID_SIDE ** (-0.5),
    )
    return jnp.stack([real_part, imag_part])


def per_device(
    coefficients,
    potential,
    slot_atom,
    slot_count,
    point_offset,
    proj_value,
    proj_strength,
    proj_count,
):
    highest = lax.Precision.HIGHEST
    cosine_lookup, sine_lookup = phase_tables()
    device = lax.axis_index("pencil")
    devices_all = lax.axis_size("pencil")
    band_total = coefficients.shape[1]
    column_local = coefficients.shape[2]
    incoming_pieces = lax.all_to_all(
        columns_to_planes(coefficients, cosine_lookup, sine_lookup),
        "pencil",
        split_axis=2,
        concat_axis=3,
        tiled=True,
    )
    real_field, imag_field = planes_to_grid(incoming_pieces, cosine_lookup, sine_lookup)
    plane_local = real_field.shape[1]
    field_row_values = 2 * band_total
    fields = jnp.stack([real_field, imag_field]).reshape(
        field_row_values, plane_local * GRID_SIDE * GRID_SIDE
    )
    coeff_width = field_row_values * NPROJ
    slot_local = slot_atom.shape[0]
    used_total = slot_count[0]
    groups_live = (used_total + 7) // 8

    def gather_group(group_index, coeffs):
        first_slot = group_index * 8
        offsets = lax.dynamic_slice_in_dim(point_offset, first_slot, 8, 0)
        values = lax.dynamic_slice_in_dim(proj_value, first_slot, 8, 0)
        live_slot = first_slot + jnp.arange(8, dtype=jnp.int32) < used_total
        picked = fields[:, offsets]
        slot_terms = jnp.einsum("mst,spt->smp", picked, values, precision=highest)
        slot_terms = jnp.where(live_slot[:, None, None], slot_terms, 0.0).reshape(8, coeff_width)
        return lax.dynamic_update_slice_in_dim(coeffs, slot_terms, first_slot, 0)

    coeffs = lax.fori_loop(
        0, groups_live, gather_group, jnp.zeros((slot_local, coeff_width), jnp.float32)
    )
    atom_total = proj_strength.shape[0]
    atom_dev = atom_total // devices_all
    column_proj = jnp.arange(coeff_width, dtype=jnp.int32) % NPROJ
    proj_mask_all = column_proj[None, :] < proj_count[:, None]
    strength_all = jnp.tile(proj_strength, (1, field_row_values))
    window_size = 2 * REACH + 1
    home_block = slot_atom // atom_dev
    relative = (home_block - device + REACH) % devices_all
    window_index = relative * atom_dev + slot_atom % atom_dev
    onehot = (
        window_index[:, None] == jnp.arange(window_size * atom_dev, dtype=jnp.int32)[None, :]
    ).astype(jnp.float32)
    partial_sum = jnp.dot(onehot.T, coeffs, precision=highest).reshape(
        window_size, atom_dev, coeff_width
    )
    mask_home = lax.dynamic_slice_in_dim(proj_mask_all, device * atom_dev, atom_dev, 0)
    strength_home = lax.dynamic_slice_in_dim(strength_all, device * atom_dev, atom_dev, 0)
    totals = partial_sum[REACH]
    for offset in range(-REACH, REACH + 1):
        if offset != 0:
            totals = totals + passed_along(partial_sum[REACH + offset], "pencil", offset)
    becp_home = jnp.where(mask_home, totals, 0.0)
    energy_home = becp_home * strength_home
    pieces = []
    for offset in range(-REACH, REACH + 1):
        if offset == 0:
            pieces.append(energy_home)
        else:
            pieces.append(passed_along(energy_home, "pencil", -offset))
    window = jnp.concatenate(pieces, 0)
    slot_energy = jnp.dot(onehot, window, precision=highest)

    def apply_group(group_index, projected):
        first_slot = group_index * 8
        offsets = lax.dynamic_slice_in_dim(point_offset, first_slot, 8, 0)
        values = lax.dynamic_slice_in_dim(proj_value, first_slot, 8, 0)
        live_slot = first_slot + jnp.arange(8, dtype=jnp.int32) < used_total
        energy = lax.dynamic_slice_in_dim(slot_energy, first_slot, 8, 0).reshape(
            8, field_row_values, NPROJ
        )
        energy = jnp.where(live_slot[:, None, None], energy, 0.0)
        slot_terms = jnp.einsum("smp,spt->mst", energy, values, precision=highest)
        return projected.at[:, offsets].add(slot_terms)

    projected = lax.fori_loop(0, groups_live, apply_group, jnp.zeros_like(fields))
    applied = potential.reshape(1, -1) * fields + projected
    applied = applied.reshape(2, band_total, plane_local, GRID_SIDE, GRID_SIDE)
    incoming_pieces = lax.all_to_all(
        grid_to_planes(applied[0], applied[1], cosine_lookup, sine_lookup),
        "pencil",
        split_axis=3,
        concat_axis=2,
        tiled=True,
    )
    transformed = planes_to_columns(incoming_pieces, cosine_lookup, sine_lookup)
    columns = device * column_local + jnp.arange(column_local, dtype=jnp.int32)
    freq_x = columns // WAVE_CUTOFF - WAVE_CUTOFF // 2
    freq_y = columns % WAVE_CUTOFF - WAVE_CUTOFF // 2
    freq_z = jnp.arange(WAVE_CUTOFF, dtype=jnp.int32) - WAVE_CUTOFF // 2
    squared = (freq_x * freq_x + freq_y * freq_y)[:, None] + (freq_z * freq_z)[None, :]
    kinetic = 6.0 / (WAVE_CUTOFF * WAVE_CUTOFF) * squared.astype(jnp.float32)
    applied_coefficients = transformed + kinetic[None, None] * coefficients
    return (applied_coefficients, becp_home)


MIB = 1024 * 1024
BF = jnp.bfloat16


def split_table(table, axis):
    high = table.astype(ml_dtypes.bfloat16)
    low = (table - high.astype(np.float64)).astype(ml_dtypes.bfloat16)
    return jnp.asarray(np.concatenate([high, high, low], axis))


def split_data(data, axis):
    high = data.astype(BF)
    low = (data - high.astype(jnp.float32)).astype(BF)
    return jnp.concatenate([high, low, high], axis)


def host_tables(devices):
    frequency = np.arange(WAVE_CUTOFF) - WAVE_CUTOFF // 2
    turns = (np.arange(GRID_SIDE)[:, None] * frequency[None, :]) % GRID_SIDE
    angle = 2.0 * np.pi / GRID_SIDE * turns
    cosine, sine = np.cos(angle), np.sin(angle)
    fwd = np.block([[cosine, -sine], [sine, cosine]]) * WAVE_CUTOFF ** (-0.5)
    bwd = np.block([[cosine.T, sine.T], [-sine.T, cosine.T]]) * GRID_SIDE ** (-0.5)
    width = WAVE_CUTOFF // devices
    order = np.arange(WAVE_CUTOFF).reshape(devices, width).T.reshape(-1)
    order = np.concatenate([order, WAVE_CUTOFF + order])
    return fwd, bwd, fwd[:, order], bwd[order, :]


def mm(left, right):
    return jnp.dot(left, right, preferred_element_type=jnp.float32)


def z_forward(coefficients, table, devices, width, zl):
    bands = coefficients.shape[1]

    def body(x_ref, t_ref, o_ref):
        x = jnp.concatenate([x_ref[0, 0], x_ref[1, 0]], 1)
        out = lax.dot_general(
            t_ref[...], split_data(x, 1), (((1,), (1,)), ((), ())),
            preferred_element_type=jnp.float32,
        )
        for c in range(2):
            for k in range(width):
                piece = out[c * GRID_SIDE:(c + 1) * GRID_SIDE, k * 128:(k + 1) * 128]
                o_ref[:, 0, c, k] = piece.reshape(devices, zl, 128)

    return pl.pallas_call(
        body,
        grid=(bands,),
        in_specs=[
            pl.BlockSpec((2, 1, width * 128, 128), lambda b: (0, b, 0, 0)),
            pl.BlockSpec(table.shape, lambda b: (0, 0)),
        ],
        out_specs=pl.BlockSpec((devices, 1, 2, width, zl, 128), lambda b: (0, b, 0, 0, 0, 0)),
        out_shape=jax.ShapeDtypeStruct((devices, bands, 2, width, zl, 128), jnp.float32),
        compiler_params=pltpu.CompilerParams(vmem_limit_bytes=40 * MIB),
        name="z_forward",
    )(coefficients, table)


def grid_and_gather(pieces, x_table, y_table, points, used, devices, width, zl, slots, npts):
    bands = pieces.shape[1]
    rows = 2 * width * zl
    pieces = pieces.reshape(devices, bands, rows, 128)
    total = zl * 4 * GRID_SIDE * 8

    def body(points_ref, used_ref, r_ref, x_ref, y_ref, u_ref, g_ref):
        band = pl.program_id(0)
        flat = r_ref.reshape(devices * rows, 128)

        @pl.loop(0, zl // 2)
        def _(pair):
            sides = []
            for half in range(2):
                z = pair * 2 + half
                sides.append(jnp.concatenate(
                    [flat[pl.ds(j * zl + z, devices, stride=rows), :] for j in range(2 * width)], 0
                ))
            first = mm(x_ref[...], split_data(jnp.concatenate(sides, 1), 0))
            for half in range(2):
                z = pair * 2 + half
                lanes = slice(half * 128, half * 128 + 128)
                left = jnp.concatenate([first[:GRID_SIDE, lanes], first[GRID_SIDE:, lanes]], 1)
                second = mm(split_data(left, 1), y_ref[...])
                for c in range(2):
                    for yh in range(2):
                        base = ((z * 2 + yh) * 2 + c) * GRID_SIDE * 8 + band
                        u_ref[pl.ds(base, GRID_SIDE, stride=8), :] = second[
                            :, c * 256 + yh * 128:c * 256 + yh * 128 + 128
                        ]

        @pl.when(band == bands - 1)
        def _():
            lane = lax.broadcasted_iota(jnp.int32, (8, 128), 1)

            @pl.loop(0, used_ref[0])
            def _(slot):
                for part in range(npts // 128):
                    first_point = slot * npts + part * 128

                    def step(i, carry):
                        real, imag = carry
                        for q in range(16):
                            t = i * 16 + q
                            p = points_ref[first_point + t]
                            row = pl.multiple_of((p >> 7) * 8, 8)
                            shift = (t - p) & 127
                            here = lane == t
                            a = pltpu.roll(u_ref[pl.ds(row, 8), :], shift, 1)
                            b = pltpu.roll(u_ref[pl.ds(row + GRID_SIDE * 8, 8), :], shift, 1)
                            real = jnp.where(here, a, real)
                            imag = jnp.where(here, b, imag)
                        return real, imag

                    zero = jnp.zeros((8, 128), jnp.float32)
                    real, imag = lax.fori_loop(0, 8, step, (zero, zero))
                    g_ref[slot, 0:8, part * 128:(part + 1) * 128] = real
                    g_ref[slot, 8:16, part * 128:(part + 1) * 128] = imag

    return pl.pallas_call(
        body,
        grid=(bands,),
        in_specs=[
            pl.BlockSpec(memory_space=pltpu.SMEM),
            pl.BlockSpec(memory_space=pltpu.SMEM),
            pl.BlockSpec((devices, 1, rows, 128), lambda b: (0, b, 0, 0)),
            pl.BlockSpec(x_table.shape, lambda b: (0, 0)),
            pl.BlockSpec(y_table.shape, lambda b: (0, 0)),
        ],
        out_specs=[
            pl.BlockSpec((total, 128), lambda b: (0, 0), pipeline_mode=pl.Buffered(1)),
            pl.BlockSpec((slots, 16, npts), lambda b: (0, 0, 0)),
        ],
        out_shape=[
            jax.ShapeDtypeStruct((total, 128), jnp.float32),
            jax.ShapeDtypeStruct((slots, 16, npts), jnp.float32),
        ],
        compiler_params=pltpu.CompilerParams(vmem_limit_bytes=58 * MIB),
        name="grid_and_gather",
    )(points, used, pieces, x_table, y_table)


def scatter_and_back(field, pot, terms, y_table, x_table, points, used, devices, width, zl):
    slots, _, npts = terms.shape
    bands = 8
    per_z = 4 * GRID_SIDE * 8
    rows = 2 * width * bands

    def body(points_ref, used_ref, u_ref, pot_ref, terms_ref, y_ref, x_ref, o_ref, acc_ref):
        z = pl.program_id(0)

        @pl.when(z == 0)
        def _():
            lane = lax.broadcasted_iota(jnp.int32, (8, 128), 1)

            @pl.loop(0, zl * per_z // 512)
            def _(i):
                acc_ref[pl.ds(pl.multiple_of(i * 512, 512), 512), :] = jnp.zeros((512, 128), jnp.float32)

            @pl.loop(0, used_ref[0])
            def _(slot):
                for part in range(npts // 128):
                    first_point = slot * npts + part * 128
                    real = terms_ref[slot, 0:8, part * 128:(part + 1) * 128]
                    imag = terms_ref[slot, 8:16, part * 128:(part + 1) * 128]

                    @pl.loop(0, 8)
                    def _(i):
                        for q in range(16):
                            t = i * 16 + q
                            p = points_ref[first_point + t]
                            row = pl.multiple_of((p >> 7) * 8, 8)
                            shift = (p - t) & 127
                            here = lane == (p & 127)
                            a = jnp.where(here, pltpu.roll(real, shift, 1), 0.0)
                            b = jnp.where(here, pltpu.roll(imag, shift, 1), 0.0)
                            acc_ref[pl.ds(row, 8), :] += a
                            acc_ref[pl.ds(row + GRID_SIDE * 8, 8), :] += b

        flat = o_ref.reshape(devices * rows, 128)

        @pl.loop(0, bands // 2)
        def _(pair):
            sides = []
            for half in range(2):
                band = pair * 2 + half
                cols = []
                for c in range(2):
                    for yh in range(2):
                        base = (yh * 2 + c) * GRID_SIDE * 8 + band
                        cols.append(
                            u_ref[pl.ds(base, GRID_SIDE, stride=8), :] * pot_ref[0, yh]
                            + acc_ref[pl.ds(z * per_z + base, GRID_SIDE, stride=8), :]
                        )
                first = mm(split_data(jnp.concatenate(cols, 1), 1), y_ref[...])
                sides.append(jnp.concatenate([first[:, :128], first[:, 128:]], 0))
            second = mm(x_ref[...], split_data(jnp.concatenate(sides, 1), 0))
            for half in range(2):
                band = pair * 2 + half
                for j in range(2 * width):
                    flat[pl.ds(j * bands + band, devices, stride=rows), :] = second[
                        j * devices:(j + 1) * devices, half * 128:half * 128 + 128
                    ]

    return pl.pallas_call(
        body,
        grid=(zl,),
        in_specs=[
            pl.BlockSpec(memory_space=pltpu.SMEM),
            pl.BlockSpec(memory_space=pltpu.SMEM),
            pl.BlockSpec((per_z, 128), lambda z: (z, 0)),
            pl.BlockSpec((1, 2, GRID_SIDE, 128), lambda z: (z, 0, 0, 0)),
            pl.BlockSpec(terms.shape, lambda z: (0, 0, 0)),
            pl.BlockSpec(y_table.shape, lambda z: (0, 0)),
            pl.BlockSpec(x_table.shape, lambda z: (0, 0)),
        ],
        out_specs=pl.BlockSpec((devices, 1, rows, 128), lambda z: (0, z, 0, 0)),
        out_shape=jax.ShapeDtypeStruct((devices, zl, rows, 128), jnp.float32),
        scratch_shapes=[pltpu.VMEM((zl * per_z, 128), jnp.float32)],
        compiler_params=pltpu.CompilerParams(vmem_limit_bytes=60 * MIB),
        name="scatter_and_back",
    )(points, used, field, pot, terms, y_table, x_table)


def z_backward(pieces, table, coefficients, device, devices, width, zl):
    bands = 8
    rows = 2 * width * bands
    pieces = pieces.reshape(devices * zl * rows, 128)

    def body(dev_ref, r_ref, t_ref, c_ref, o_ref):
        band = pl.program_id(0)
        fy = lax.broadcasted_iota(jnp.int32, (128, 128), 0) - WAVE_CUTOFF // 2
        fz = lax.broadcasted_iota(jnp.int32, (128, 128), 1) - WAVE_CUTOFF // 2
        for k in range(width):
            data = jnp.concatenate(
                [r_ref[pl.ds((c * width + k) * bands + band, GRID_SIDE, stride=rows), :] for c in range(2)], 0
            )
            res = mm(split_data(data.T, 1), t_ref[...])
            fx = dev_ref[0] * width + k - WAVE_CUTOFF // 2
            kinetic = 6.0 / (WAVE_CUTOFF * WAVE_CUTOFF) * (fy * fy + fz * fz + fx * fx).astype(jnp.float32)
            for c in range(2):
                o_ref[c, 0, k * 128:(k + 1) * 128, :] = (
                    res[:, c * 128:(c + 1) * 128] + kinetic * c_ref[c, 0, k * 128:(k + 1) * 128, :]
                )

    spec = pl.BlockSpec((2, 1, width * 128, 128), lambda b: (0, b, 0, 0))
    return pl.pallas_call(
        body,
        grid=(bands,),
        in_specs=[
            pl.BlockSpec(memory_space=pltpu.SMEM),
            pl.BlockSpec(pieces.shape, lambda b: (0, 0), pipeline_mode=pl.Buffered(1)),
            pl.BlockSpec(table.shape, lambda b: (0, 0)),
            spec,
        ],
        out_specs=spec,
        out_shape=jax.ShapeDtypeStruct(coefficients.shape, jnp.float32),
        compiler_params=pltpu.CompilerParams(vmem_limit_bytes=48 * MIB),
        name="z_backward",
    )(device.reshape(1), pieces, table, coefficients)


def per_device_fast(
    coefficients,
    potential,
    slot_atom,
    slot_count,
    point_offset,
    proj_value,
    proj_strength,
    proj_count,
):
    highest = lax.Precision.HIGHEST
    device = lax.axis_index("pencil")
    devices = lax.axis_size("pencil")
    width = coefficients.shape[2] // WAVE_CUTOFF
    zl = potential.shape[0]
    slots, npts = point_offset.shape
    fwd, bwd, fwd_x, bwd_x = host_tables(devices)
    sent = z_forward(coefficients, split_table(fwd, 1), devices, width, zl)
    pieces = lax.all_to_all(sent, "pencil", split_axis=0, concat_axis=0, tiled=True)
    z = point_offset // (GRID_SIDE * GRID_SIDE)
    y = point_offset // GRID_SIDE % GRID_SIDE
    x = point_offset % GRID_SIDE
    points = (((z * 2 + y // 128) * 2 * GRID_SIDE + x) * 128 + y % 128).reshape(-1)
    used = slot_count
    field, picked = grid_and_gather(
        pieces, split_table(fwd_x, 1), split_table(fwd.T, 0), points, used,
        devices, width, zl, slots, npts,
    )
    live = jnp.arange(slots, dtype=jnp.int32) < used[0]
    coeffs = jnp.einsum("smt,spt->smp", picked, proj_value, precision=highest)
    coeff_width = 16 * NPROJ
    coeffs = jnp.where(live[:, None, None], coeffs, 0.0).reshape(slots, coeff_width)
    atom_dev = proj_strength.shape[0] // devices
    column_proj = jnp.arange(coeff_width, dtype=jnp.int32) % NPROJ
    window_size = 2 * REACH + 1
    relative = (slot_atom // atom_dev - device + REACH) % devices
    window_index = relative * atom_dev + slot_atom % atom_dev
    onehot = (
        window_index[:, None] == jnp.arange(window_size * atom_dev, dtype=jnp.int32)[None, :]
    ).astype(jnp.float32)
    partial_sum = jnp.dot(onehot.T, coeffs, precision=highest).reshape(
        window_size, atom_dev, coeff_width
    )
    count_home = lax.dynamic_slice_in_dim(proj_count, device * atom_dev, atom_dev, 0)
    mask_home = column_proj[None, :] < count_home[:, None]
    strength_home = jnp.tile(
        lax.dynamic_slice_in_dim(proj_strength, device * atom_dev, atom_dev, 0), (1, 16)
    )
    totals = partial_sum[REACH]
    for offset in range(-REACH, REACH + 1):
        if offset != 0:
            totals = totals + passed_along(partial_sum[REACH + offset], "pencil", offset)
    becp_home = jnp.where(mask_home, totals, 0.0)
    energy_home = becp_home * strength_home
    window = jnp.concatenate(
        [
            energy_home if offset == 0 else passed_along(energy_home, "pencil", -offset)
            for offset in range(-REACH, REACH + 1)
        ],
        0,
    )
    energy = jnp.dot(onehot, window, precision=highest).reshape(slots, 16, NPROJ)
    terms = jnp.einsum("smp,spt->smt", energy, proj_value, precision=highest)
    pot = potential.reshape(zl, 2, 128, GRID_SIDE).transpose(0, 1, 3, 2)
    back = scatter_and_back(
        field, pot, terms, split_table(bwd.T, 0), split_table(bwd_x, 1), points, used,
        devices, width, zl,
    )
    pieces = lax.all_to_all(back, "pencil", split_axis=0, concat_axis=0, tiled=True)
    applied_coefficients = z_backward(
        pieces, split_table(bwd.T, 0), coefficients, device, devices, width, zl
    )
    return (applied_coefficients, becp_home)


def per_device_any(coefficients, potential, *rest):
    whole_tiles = potential.shape[0] % 8 == 0 and coefficients.shape[1] == 8
    body = per_device_fast if whole_tiles else per_device
    return body(coefficients, potential, *rest)


def solution(mesh):
    in_specs = (
        P(None, None, "pencil", None),
        P("pencil", None, None),
        P("pencil"),
        P("pencil"),
        P("pencil", None),
        P("pencil", None, None),
        P(),
        P(),
    )
    out_specs = (P(None, None, "pencil", None), P("pencil", None))
    return jax.shard_map(
        per_device_any, mesh=mesh, in_specs=in_specs, out_specs=out_specs, check_vma=False
    )
```

```python
import math

import jax
import jax.numpy as jnp
import ml_dtypes
import numpy as np
from jax import lax
from jax.experimental import pallas as pl
from jax.experimental.pallas import tpu as pltpu
from jax.sharding import PartitionSpec as P

GRID_SIDE = 256
WAVE_CUTOFF = 128
NPROJ = 8
REACH = 2


def passed_along(block, axis, distance):
    devices = range(lax.axis_size(axis))
    route = [((i - distance) % len(devices), i) for i in devices]
    return lax.ppermute(block, axis, route)


def phase_tables():
    frequency = jnp.arange(WAVE_CUTOFF, dtype=jnp.int32) - WAVE_CUTOFF // 2
    points = jnp.arange(GRID_SIDE, dtype=jnp.int32)
    turn_count = frequency[:, None] * points[None, :] % GRID_SIDE
    phase_angles = 2.0 * math.pi / GRID_SIDE * turn_count.astype(jnp.float32)
    return (jnp.cos(phase_angles), jnp.sin(phase_angles))


def complex_step(real_part, imag_part, full_pattern, table, factor):
    stacked = jnp.stack([real_part, imag_part])
    result = jnp.einsum(full_pattern, stacked, table, precision=lax.Precision.HIGHEST)
    return (factor * result[0], factor * result[1])


def forward_dim(real_part, imag_part, full_pattern, cosine_lookup, sine_lookup, factor):
    table = jnp.stack(
        [jnp.stack([cosine_lookup, sine_lookup]), jnp.stack([-sine_lookup, cosine_lookup])]
    )
    return complex_step(real_part, imag_part, full_pattern, table, factor)


def backward_dim(real_part, imag_part, full_pattern, cosine_lookup, sine_lookup, factor):
    table = jnp.stack(
        [jnp.stack([cosine_lookup, -sine_lookup]), jnp.stack([sine_lookup, cosine_lookup])]
    )
    return complex_step(real_part, imag_part, full_pattern, table, factor)


def columns_to_planes(band_amplitudes, cosine_lookup, sine_lookup):
    real_part, imag_part = forward_dim(
        band_amplitudes[0],
        band_amplitudes[1],
        "rchw,rowa->ocah",
        cosine_lookup,
        sine_lookup,
        WAVE_CUTOFF ** (-0.5),
    )
    return jnp.stack([real_part, imag_part])


def planes_to_grid(incoming_pieces, cosine_lookup, sine_lookup):
    shape_now = incoming_pieces.shape
    real_part = incoming_pieces[0].reshape(shape_now[1], shape_now[2], WAVE_CUTOFF, WAVE_CUTOFF)
    imag_part = incoming_pieces[1].reshape(shape_now[1], shape_now[2], WAVE_CUTOFF, WAVE_CUTOFF)
    real_part, imag_part = forward_dim(
        real_part, imag_part, "rbzkj,rojy->obzky", cosine_lookup, sine_lookup, WAVE_CUTOFF ** (-0.5)
    )
    return forward_dim(
        real_part, imag_part, "rbzky,rokx->obzyx", cosine_lookup, sine_lookup, WAVE_CUTOFF ** (-0.5)
    )


def grid_to_planes(real_part, imag_part, cosine_lookup, sine_lookup):
    real_part, imag_part = backward_dim(
        real_part, imag_part, "rbzyx,rokx->obzyk", cosine_lookup, sine_lookup, GRID_SIDE ** (-0.5)
    )
    real_part, imag_part = backward_dim(
        real_part, imag_part, "rbzyk,rojy->obzkj", cosine_lookup, sine_lookup, GRID_SIDE ** (-0.5)
    )
    shape_now = real_part.shape
    return jnp.stack(
        [
            real_part.reshape(shape_now[0], shape_now[1], WAVE_CUTOFF * WAVE_CUTOFF),
            imag_part.reshape(shape_now[0], shape_now[1], WAVE_CUTOFF * WAVE_CUTOFF),
        ]
    )


def planes_to_columns(incoming_pieces, cosine_lookup, sine_lookup):
    real_part, imag_part = backward_dim(
        incoming_pieces[0],
        incoming_pieces[1],
        "runv,rotn->ouvt",
        cosine_lookup,
        sine_lookup,
        GRID_SIDE ** (-0.5),
    )
    return jnp.stack([real_part, imag_part])


def per_device(
    coefficients,
    potential,
    slot_atom,
    slot_count,
    point_offset,
    proj_value,
    proj_strength,
    proj_count,
):
    highest = lax.Precision.HIGHEST
    cosine_lookup, sine_lookup = phase_tables()
    device = lax.axis_index("pencil")
    devices_all = lax.axis_size("pencil")
    band_total = coefficients.shape[1]
    column_local = coefficients.shape[2]
    incoming_pieces = lax.all_to_all(
        columns_to_planes(coefficients, cosine_lookup, sine_lookup),
        "pencil",
        split_axis=2,
        concat_axis=3,
        tiled=True,
    )
    real_field, imag_field = planes_to_grid(incoming_pieces, cosine_lookup, sine_lookup)
    plane_local = real_field.shape[1]
    field_row_values = 2 * band_total
    fields = jnp.stack([real_field, imag_field]).reshape(
        field_row_values, plane_local * GRID_SIDE * GRID_SIDE
    )
    coeff_width = field_row_values * NPROJ
    slot_local = slot_atom.shape[0]
    used_total = slot_count[0]
    groups_live = (used_total + 7) // 8

    def gather_group(group_index, coeffs):
        first_slot = group_index * 8
        offsets = lax.dynamic_slice_in_dim(point_offset, first_slot, 8, 0)
        values = lax.dynamic_slice_in_dim(proj_value, first_slot, 8, 0)
        live_slot = first_slot + jnp.arange(8, dtype=jnp.int32) < used_total
        picked = fields[:, offsets]
        slot_terms = jnp.einsum("mst,spt->smp", picked, values, precision=highest)
        slot_terms = jnp.where(live_slot[:, None, None], slot_terms, 0.0).reshape(8, coeff_width)
        return lax.dynamic_update_slice_in_dim(coeffs, slot_terms, first_slot, 0)

    coeffs = lax.fori_loop(
        0, groups_live, gather_group, jnp.zeros((slot_local, coeff_width), jnp.float32)
    )
    atom_total = proj_strength.shape[0]
    atom_dev = atom_total // devices_all
    column_proj = jnp.arange(coeff_width, dtype=jnp.int32) % NPROJ
    proj_mask_all = column_proj[None, :] < proj_count[:, None]
    strength_all = jnp.tile(proj_strength, (1, field_row_values))
    window_size = 2 * REACH + 1
    home_block = slot_atom // atom_dev
    relative = (home_block - device + REACH) % devices_all
    window_index = relative * atom_dev + slot_atom % atom_dev
    onehot = (
        window_index[:, None] == jnp.arange(window_size * atom_dev, dtype=jnp.int32)[None, :]
    ).astype(jnp.float32)
    partial_sum = jnp.dot(onehot.T, coeffs, precision=highest).reshape(
        window_size, atom_dev, coeff_width
    )
    mask_home = lax.dynamic_slice_in_dim(proj_mask_all, device * atom_dev, atom_dev, 0)
    strength_home = lax.dynamic_slice_in_dim(strength_all, device * atom_dev, atom_dev, 0)
    totals = partial_sum[REACH]
    for offset in range(-REACH, REACH + 1):
        if offset != 0:
            totals = totals + passed_along(partial_sum[REACH + offset], "pencil", offset)
    becp_home = jnp.where(mask_home, totals, 0.0)
    energy_home = becp_home * strength_home
    pieces = []
    for offset in range(-REACH, REACH + 1):
        if offset == 0:
            pieces.append(energy_home)
        else:
            pieces.append(passed_along(energy_home, "pencil", -offset))
    window = jnp.concatenate(pieces, 0)
    slot_energy = jnp.dot(onehot, window, precision=highest)

    def apply_group(group_index, projected):
        first_slot = group_index * 8
        offsets = lax.dynamic_slice_in_dim(point_offset, first_slot, 8, 0)
        values = lax.dynamic_slice_in_dim(proj_value, first_slot, 8, 0)
        live_slot = first_slot + jnp.arange(8, dtype=jnp.int32) < used_total
        energy = lax.dynamic_slice_in_dim(slot_energy, first_slot, 8, 0).reshape(
            8, field_row_values, NPROJ
        )
        energy = jnp.where(live_slot[:, None, None], energy, 0.0)
        slot_terms = jnp.einsum("smp,spt->mst", energy, values, precision=highest)
        return projected.at[:, offsets].add(slot_terms)

    projected = lax.fori_loop(0, groups_live, apply_group, jnp.zeros_like(fields))
    applied = potential.reshape(1, -1) * fields + projected
    applied = applied.reshape(2, band_total, plane_local, GRID_SIDE, GRID_SIDE)
    incoming_pieces = lax.all_to_all(
        grid_to_planes(applied[0], applied[1], cosine_lookup, sine_lookup),
        "pencil",
        split_axis=3,
        concat_axis=2,
        tiled=True,
    )
    transformed = planes_to_columns(incoming_pieces, cosine_lookup, sine_lookup)
    columns = device * column_local + jnp.arange(column_local, dtype=jnp.int32)
    freq_x = columns // WAVE_CUTOFF - WAVE_CUTOFF // 2
    freq_y = columns % WAVE_CUTOFF - WAVE_CUTOFF // 2
    freq_z = jnp.arange(WAVE_CUTOFF, dtype=jnp.int32) - WAVE_CUTOFF // 2
    squared = (freq_x * freq_x + freq_y * freq_y)[:, None] + (freq_z * freq_z)[None, :]
    kinetic = 6.0 / (WAVE_CUTOFF * WAVE_CUTOFF) * squared.astype(jnp.float32)
    applied_coefficients = transformed + kinetic[None, None] * coefficients
    return (applied_coefficients, becp_home)


MIB = 1024 * 1024
BF = jnp.bfloat16
HALF = 4


def cost(flops, moved):
    return pl.CostEstimate(flops=flops, bytes_accessed=moved, transcendentals=0)


def split_table(table, axis):
    high = table.astype(ml_dtypes.bfloat16)
    low = (table - high.astype(np.float64)).astype(ml_dtypes.bfloat16)
    return jnp.asarray(np.concatenate([high, high, low], axis))


def split_data(data, axis):
    high = data.astype(BF)
    low = (data - high.astype(jnp.float32)).astype(BF)
    return jnp.concatenate([high, low, high], axis)


def host_tables(devices):
    frequency = np.arange(WAVE_CUTOFF) - WAVE_CUTOFF // 2
    turns = (np.arange(GRID_SIDE)[:, None] * frequency[None, :]) % GRID_SIDE
    angle = 2.0 * np.pi / GRID_SIDE * turns
    cosine, sine = np.cos(angle), np.sin(angle)
    fwd = np.block([[cosine, -sine], [sine, cosine]]) * WAVE_CUTOFF ** (-0.5)
    bwd = np.block([[cosine.T, sine.T], [-sine.T, cosine.T]]) * GRID_SIDE ** (-0.5)
    width = WAVE_CUTOFF // devices
    order = np.arange(WAVE_CUTOFF).reshape(devices, width).T.reshape(-1)
    order = np.concatenate([order, WAVE_CUTOFF + order])
    return fwd, bwd, fwd[:, order], bwd[order, :]


def mm(left, right):
    return jnp.dot(left, right, preferred_element_type=jnp.float32)


def z_forward(coefficients, table, part, devices, width, zl):
    bands = HALF

    def body(x_ref, t_ref, o_ref):
        x = jnp.concatenate([x_ref[0, 0], x_ref[1, 0]], 1)
        out = lax.dot_general(
            t_ref[...], split_data(x, 1), (((1,), (1,)), ((), ())),
            preferred_element_type=jnp.float32,
        )
        for c in range(2):
            for k in range(width):
                piece = out[c * GRID_SIDE:(c + 1) * GRID_SIDE, k * 128:(k + 1) * 128]
                o_ref[:, 0, c, k] = piece.reshape(devices, zl, 128)

    return pl.pallas_call(
        body,
        grid=(bands,),
        in_specs=[
            pl.BlockSpec((2, 1, width * 128, 128), lambda b: (0, b + part * HALF, 0, 0)),
            pl.BlockSpec(table.shape, lambda b: (0, 0)),
        ],
        out_specs=pl.BlockSpec((devices, 1, 2, width, zl, 128), lambda b: (0, b, 0, 0, 0, 0)),
        out_shape=jax.ShapeDtypeStruct((devices, bands, 2, width, zl, 128), jnp.float32),
        compiler_params=pltpu.CompilerParams(vmem_limit_bytes=32 * MIB),
        cost_estimate=cost(3 * 2**30, 8 * MIB),
        name="z_forward",
    )(coefficients, table)


def grid_and_gather(pieces, x_table, y_table, point_rows, shifts, used, devices, width, zl, slots, npts):
    bands = pieces.shape[1]
    rows = 2 * width * zl
    pieces = pieces.reshape(devices, bands, rows, 128)
    total = zl * 2 * GRID_SIDE * 8

    def body(rows_ref, shifts_ref, used_ref, r_ref, x_ref, y_ref, u_ref, g_ref):
        band = pl.program_id(0)
        flat = r_ref.reshape(devices * rows, 128)

        @pl.loop(0, zl // 2)
        def _(pair):
            sides = []
            for half in range(2):
                z = pair * 2 + half
                sides.append(jnp.concatenate(
                    [flat[pl.ds(j * zl + z, devices, stride=rows), :] for j in range(2 * width)], 0
                ))
            first = mm(x_ref[...], split_data(jnp.concatenate(sides, 1), 0))
            for half in range(2):
                z = pair * 2 + half
                lanes = slice(half * 128, half * 128 + 128)
                left = jnp.concatenate([first[:GRID_SIDE, lanes], first[GRID_SIDE:, lanes]], 1)
                second = mm(split_data(left, 1), y_ref[...])
                for c in range(2):
                    for yh in range(2):
                        base = (z * 2 + yh) * GRID_SIDE * 8 + c * HALF + band
                        u_ref[pl.ds(base, GRID_SIDE, stride=8), :] = second[
                            :, c * 256 + yh * 128:c * 256 + yh * 128 + 128
                        ]

        @pl.when(band == bands - 1)
        def _():
            lane = lax.broadcasted_iota(jnp.int32, (8, 128), 1)

            @pl.loop(0, used_ref[0] * (npts // 128))
            def _(group):
                first_point = group * 128
                sums = [jnp.zeros((8, 128), jnp.float32) for _ in range(4)]
                for t in range(128):
                    row = pl.multiple_of(rows_ref[first_point + t], 8)
                    tile = pltpu.roll(u_ref[pl.ds(row, 8), :], shifts_ref[first_point + t], 1)
                    sums[t % 4] = jnp.where(lane == t, tile, sums[t % 4])
                g_ref[group] = (sums[0] + sums[1]) + (sums[2] + sums[3])

    return pl.pallas_call(
        body,
        grid=(bands,),
        in_specs=[
            pl.BlockSpec(memory_space=pltpu.SMEM),
            pl.BlockSpec(memory_space=pltpu.SMEM),
            pl.BlockSpec(memory_space=pltpu.SMEM),
            pl.BlockSpec((devices, 1, rows, 128), lambda b: (0, b, 0, 0)),
            pl.BlockSpec(x_table.shape, lambda b: (0, 0)),
            pl.BlockSpec(y_table.shape, lambda b: (0, 0)),
        ],
        out_specs=[
            pl.BlockSpec((total, 128), lambda b: (0, 0), pipeline_mode=pl.Buffered(1)),
            pl.BlockSpec((slots * npts // 128, 8, 128), lambda b: (0, 0, 0)),
        ],
        out_shape=[
            jax.ShapeDtypeStruct((total, 128), jnp.float32),
            jax.ShapeDtypeStruct((slots * npts // 128, 8, 128), jnp.float32),
        ],
        compiler_params=pltpu.CompilerParams(vmem_limit_bytes=32 * MIB),
        cost_estimate=cost(12 * 2**30, 192 * MIB),
        name="grid_and_gather",
    )(point_rows, shifts, used, pieces, x_table, y_table)


def scatter_and_back(field, pot, terms, y_table, x_table, point_rows, shifts, used, devices, width, zl):
    slots, _, npts = terms.shape
    bands = HALF
    per_z = 2 * GRID_SIDE * 8
    rows = 2 * width * bands

    def body(rows_ref, shifts_ref, used_ref, u_ref, pot_ref, terms_ref, y_ref, x_ref, o_ref, acc_ref):
        z = pl.program_id(0)

        @pl.when(z == 0)
        def _():
            lane = lax.broadcasted_iota(jnp.int32, (8, 128), 1)

            @pl.loop(0, zl * per_z // 512)
            def _(i):
                acc_ref[pl.ds(pl.multiple_of(i * 512, 512), 512), :] = jnp.zeros((512, 128), jnp.float32)

            @pl.loop(0, used_ref[0])
            def _(slot):
                for part in range(npts // 128):
                    first_point = slot * npts + part * 128
                    term = terms_ref[slot, :, part * 128:(part + 1) * 128]
                    for t in range(128):
                        row = pl.multiple_of(rows_ref[first_point + t], 8)
                        alone = jnp.where(lane == t, term, 0.0)
                        acc_ref[pl.ds(row, 8), :] += pltpu.roll(alone, shifts_ref[first_point + t], 1)

        flat = o_ref.reshape(devices * rows, 128)

        @pl.loop(0, bands // 2)
        def _(pair):
            sides = []
            for half in range(2):
                band = pair * 2 + half
                cols = []
                for c in range(2):
                    for yh in range(2):
                        base = yh * GRID_SIDE * 8 + c * HALF + band
                        cols.append(
                            u_ref[pl.ds(base, GRID_SIDE, stride=8), :] * pot_ref[0, yh]
                            + acc_ref[pl.ds(z * per_z + base, GRID_SIDE, stride=8), :]
                        )
                first = mm(split_data(jnp.concatenate(cols, 1), 1), y_ref[...])
                sides.append(jnp.concatenate([first[:, :128], first[:, 128:]], 0))
            second = mm(x_ref[...], split_data(jnp.concatenate(sides, 1), 0))
            for half in range(2):
                band = pair * 2 + half
                for j in range(2 * width):
                    flat[pl.ds((j % width * 2 + j // width) * bands + band, devices, stride=rows), :] = second[
                        j * devices:(j + 1) * devices, half * 128:half * 128 + 128
                    ]

    return pl.pallas_call(
        body,
        grid=(zl,),
        in_specs=[
            pl.BlockSpec(memory_space=pltpu.SMEM),
            pl.BlockSpec(memory_space=pltpu.SMEM),
            pl.BlockSpec(memory_space=pltpu.SMEM),
            pl.BlockSpec((per_z, 128), lambda z: (z, 0)),
            pl.BlockSpec((1, 2, GRID_SIDE, 128), lambda z: (z, 0, 0, 0)),
            pl.BlockSpec(terms.shape, lambda z: (0, 0, 0)),
            pl.BlockSpec(y_table.shape, lambda z: (0, 0)),
            pl.BlockSpec(x_table.shape, lambda z: (0, 0)),
        ],
        out_specs=pl.BlockSpec((devices, 1, rows, 128), lambda z: (0, z, 0, 0)),
        out_shape=jax.ShapeDtypeStruct((devices, zl, rows, 128), jnp.float32),
        scratch_shapes=[pltpu.VMEM((zl * per_z, 128), jnp.float32)],
        compiler_params=pltpu.CompilerParams(vmem_limit_bytes=36 * MIB),
        cost_estimate=cost(12 * 2**30, 256 * MIB),
        name="scatter_and_back",
    )(point_rows, shifts, used, field, pot, terms, y_table, x_table)


def z_backward(pieces, table, coefficients, before, part, device, devices, width, zl):
    bands = HALF
    rows = 2 * width * bands
    pieces = pieces.reshape(devices * zl * rows, 128)

    def body(dev_ref, r_ref, t_ref, c_ref, *rest):
        o_ref = rest[-1]
        band = pl.program_id(0)
        fy = lax.broadcasted_iota(jnp.int32, (128, 128), 0) - WAVE_CUTOFF // 2
        fz = lax.broadcasted_iota(jnp.int32, (128, 128), 1) - WAVE_CUTOFF // 2
        for k in range(width):
            data = jnp.concatenate(
                [r_ref[pl.ds((k * 2 + c) * bands + band, GRID_SIDE, stride=rows), :] for c in range(2)], 0
            )
            res = mm(split_data(data.T, 1), t_ref[...])
            fx = dev_ref[0] * width + k - WAVE_CUTOFF // 2
            kinetic = 6.0 / (WAVE_CUTOFF * WAVE_CUTOFF) * (fy * fy + fz * fz + fx * fx).astype(jnp.float32)
            for c in range(2):
                o_ref[c, 0, k * 128:(k + 1) * 128, :] = (
                    res[:, c * 128:(c + 1) * 128] + kinetic * c_ref[c, 0, k * 128:(k + 1) * 128, :]
                )

    spec = pl.BlockSpec((2, 1, width * 128, 128), lambda b: (0, b + part * HALF, 0, 0))
    in_specs = [
        pl.BlockSpec(memory_space=pltpu.SMEM),
        pl.BlockSpec(pieces.shape, lambda b: (0, 0), pipeline_mode=pl.Buffered(1)),
        pl.BlockSpec(table.shape, lambda b: (0, 0)),
        spec,
    ]
    operands = [device.reshape(1), pieces, table, coefficients]
    aliases = {}
    if before is not None:
        in_specs.append(pl.BlockSpec(memory_space=pl.ANY))
        operands.append(before)
        aliases = {4: 0}
    return pl.pallas_call(
        body,
        grid=(bands,),
        in_specs=in_specs,
        out_specs=spec,
        out_shape=jax.ShapeDtypeStruct(coefficients.shape, jnp.float32),
        input_output_aliases=aliases,
        compiler_params=pltpu.CompilerParams(vmem_limit_bytes=32 * MIB),
        cost_estimate=cost(3 * 2**30, 24 * MIB),
        name="z_backward",
    )(*operands)


def per_device_fast(
    coefficients,
    potential,
    slot_atom,
    slot_count,
    point_offset,
    proj_value,
    proj_strength,
    proj_count,
):
    highest = lax.Precision.HIGHEST
    device = lax.axis_index("pencil")
    devices = lax.axis_size("pencil")
    width = coefficients.shape[2] // WAVE_CUTOFF
    zl = potential.shape[0]
    slots, npts = point_offset.shape
    fwd, bwd, fwd_x, bwd_x = host_tables(devices)
    fwd_left = split_table(fwd, 1)
    sent = [z_forward(coefficients, fwd_left, part, devices, width, zl) for part in range(2)]
    first = lax.all_to_all(sent[0], "pencil", split_axis=0, concat_axis=0, tiled=True)
    first, later = lax.optimization_barrier((first, sent[1]))
    second = lax.all_to_all(later, "pencil", split_axis=0, concat_axis=0, tiled=True)
    z = point_offset // (GRID_SIDE * GRID_SIDE)
    y = point_offset // GRID_SIDE % GRID_SIDE
    x = point_offset % GRID_SIDE
    point_rows = (((z * 2 + y // 128) * GRID_SIDE + x) * 8).reshape(-1)
    turn = y % 128 - jnp.arange(npts, dtype=jnp.int32) % 128
    shifts_in = (-turn % 128).reshape(-1)
    shifts_out = (turn % 128).reshape(-1)
    used = slot_count
    live = jnp.arange(slots, dtype=jnp.int32) < used[0]
    coeff_width = 16 * NPROJ
    fields = []
    parts = []
    for pieces in (first, second):
        field, picked = grid_and_gather(
            pieces, split_table(fwd_x, 1), split_table(fwd.T, 0), point_rows, shifts_in, used,
            devices, width, zl, slots, npts,
        )
        fields.append(field)
        picked = picked.reshape(slots, npts // 128, 8, 128)
        values = proj_value.reshape(slots, NPROJ, npts // 128, 128)
        part = jnp.einsum("shmt,spht->smp", picked, values, precision=highest)
        parts.append(part.reshape(slots, 2, HALF, NPROJ))
    coeffs = jnp.concatenate(parts, 2)
    coeffs = jnp.where(live[:, None, None, None], coeffs, 0.0).reshape(slots, coeff_width)
    atom_dev = proj_strength.shape[0] // devices
    column_proj = jnp.arange(coeff_width, dtype=jnp.int32) % NPROJ
    window_size = 2 * REACH + 1
    relative = (slot_atom // atom_dev - device + REACH) % devices
    window_index = relative * atom_dev + slot_atom % atom_dev
    onehot = (
        window_index[:, None] == jnp.arange(window_size * atom_dev, dtype=jnp.int32)[None, :]
    ).astype(jnp.float32)
    partial_sum = jnp.dot(onehot.T, coeffs, precision=highest).reshape(
        window_size, atom_dev, coeff_width
    )
    count_home = lax.dynamic_slice_in_dim(proj_count, device * atom_dev, atom_dev, 0)
    mask_home = column_proj[None, :] < count_home[:, None]
    strength_home = jnp.tile(
        lax.dynamic_slice_in_dim(proj_strength, device * atom_dev, atom_dev, 0), (1, 16)
    )
    totals = partial_sum[REACH]
    for offset in range(-REACH, REACH + 1):
        if offset != 0:
            totals = totals + passed_along(partial_sum[REACH + offset], "pencil", offset)
    becp_home = jnp.where(mask_home, totals, 0.0)
    energy_home = becp_home * strength_home
    window = jnp.concatenate(
        [
            energy_home if offset == 0 else passed_along(energy_home, "pencil", -offset)
            for offset in range(-REACH, REACH + 1)
        ],
        0,
    )
    energy = jnp.dot(onehot, window, precision=highest).reshape(slots, 2, 2, HALF, NPROJ)
    pot = potential.reshape(zl, 2, 128, GRID_SIDE).transpose(0, 1, 3, 2)
    bwd_right = split_table(bwd.T, 0)
    backs = []
    for part in range(2):
        terms = jnp.einsum(
            "smp,spt->smt", energy[:, :, part].reshape(slots, 8, NPROJ), proj_value, precision=highest
        )
        if part == 1:
            backs[0], terms = lax.optimization_barrier((backs[0], terms))
        back = scatter_and_back(
            fields[part], pot, terms, bwd_right, split_table(bwd_x, 1), point_rows, shifts_out, used,
            devices, width, zl,
        )
        backs.append(back)
    backs = [
        lax.all_to_all(back, "pencil", split_axis=0, concat_axis=0, tiled=True) for back in backs
    ]
    applied_coefficients = None
    for part in range(2):
        applied_coefficients = z_backward(
            backs[part], bwd_right, coefficients, applied_coefficients, part, device, devices, width, zl
        )
    return (applied_coefficients, becp_home)


def per_device_any(coefficients, potential, *rest):
    whole_tiles = potential.shape[0] % 8 == 0 and coefficients.shape[1] == 8
    body = per_device_fast if whole_tiles else per_device
    return body(coefficients, potential, *rest)


def solution(mesh):
    in_specs = (
        P(None, None, "pencil", None),
        P("pencil", None, None),
        P("pencil"),
        P("pencil"),
        P("pencil", None),
        P("pencil", None, None),
        P(),
        P(),
    )
    out_specs = (P(None, None, "pencil", None), P("pencil", None))
    return jax.shard_map(
        per_device_any, mesh=mesh, in_specs=in_specs, out_specs=out_specs, check_vma=False
    )
```
